32 devices in a mesh: aux: 4 (over z), orb: 8 (over y, x, core).
Axes of the slice: x: 2, y: 2, z: 4, core: 2. Of those that a mesh axis runs over, the one named last changes fastest.
Arguments:
- three_centre: bfloat16 [256, 3, 3, 16, 128, 128], P(('aux', 'orb')), may hold values from -0.59765625 to 0.59765625
- block_lists: int32 [256, 3], P(('aux', 'orb')), may hold values from 0 to 7, as said below
- occupied: bfloat16 [1024, 512], P('orb'), may hold values from -0.1796875 to 0.1796875
Outputs:
- exchange_band: float32 [8, 128, 896], P('orb', 'aux')
The draws below stay inside these ranges and needn't reach their ends.
Inputs may be any that keep to these rules, and one draw needn't show every extreme that they name: Each row of block_lists holds 3 increasing basis blocks that lie within 4 consecutive blocks. The auxiliary blocks held at orb index o list only basis blocks from o - 4 to o + 3.
All inputs are finite; a program needn't handle non-finite values.
Results may differ from the reference program's by a relative error of at most 0.0003.
Values may be sent and summed in bfloat16 or wider, within the bound.
No kernel may reach another device: no remote copies, remote signals or barrier semaphores. Data moves between devices by JAX's collectives and lax.ppermute only.
A program may use at most 128 MiB of HBM per device.

```python
import jax
import jax.numpy as jnp
from jax import lax

OCC = 512
AB = 16
BLK = 128
SB = 3
NB_DEV = 1
NB = 8
BASIS = 1024
NAB = 256
BAND = 7
N_ORB = 8
DEVICES = 32


def draw_block_lists(key, part):
    key = jax.random.fold_in(key, 7)
    first_key, second_key = jax.random.split(key)
    per_device = NAB // DEVICES
    blocks = jnp.arange(NAB, dtype=jnp.int32)
    owner = blocks // per_device % N_ORB
    jitter = jax.random.randint(first_key, (NAB,), -SB - 1, NB_DEV, dtype=jnp.int32)
    starts = jnp.clip(owner * NB_DEV + jitter, 0, NB - SB - 1).astype(jnp.int32)
    skipped = jax.random.randint(second_key, (NAB,), 0, SB + 1, dtype=jnp.int32)
    middle = N_ORB // 2
    low_row = middle * per_device
    high_row = (N_ORB + middle) * per_device
    last_row = (N_ORB - 1) * per_device
    starts = starts.at[0].set(0).at[low_row].set(middle * NB_DEV - SB - 1)
    starts = starts.at[high_row].set((middle + 1) * NB_DEV - 1).at[last_row].set(NB - SB - 1)
    skipped = skipped.at[0].set(1).at[low_row].set(SB).at[high_row].set(0).at[last_row].set(0)
    steps_up = jnp.arange(SB, dtype=jnp.int32)[None, :]
    offsets = steps_up + (steps_up >= skipped[:, None]).astype(jnp.int32)
    return (starts[:, None] + offsets).astype(jnp.int32)


def level_of(rng, dims, shards, least, largest):
    gain = 1.0
    for dim, shards_of in shards:
        draws = jax.random.uniform(jax.random.fold_in(jax.random.fold_in(rng, 6), dim), (shards_of,), jnp.float32, least / len(shards), largest / len(shards))
        gain = gain * jnp.repeat(jnp.exp(draws), dims[dim] // shards_of).reshape((-1,) + (1,) * (len(dims) - 1 - dim))
    return gain


def bell_draw(key, dims, width, bound, cuts=(), kind=jnp.bfloat16):
    entries = jax.random.normal(key, dims, jnp.float32) * width
    if len(cuts) > 0:
        entries = level_of(key, dims, cuts, -0.22, 0.18) * entries
    return jnp.clip(entries, min=-bound, max=bound).astype(kind)


def setup_inputs(seed: int = 0) -> dict:
    splits = jax.random.split(jax.random.key(seed), 4)
    return {
        "three_centre": bell_draw(splits[0], (NAB, SB, SB, AB, BLK, BLK), 0.1, 0.59765625, ((0, 32),)),
        "block_lists": draw_block_lists(jax.random.fold_in(splits[3], 71), 0),
        "occupied": bell_draw(splits[2], (BASIS, OCC), 0.03, 0.1796875, ((0, 8),)),
    }


def reference(three_centre, block_lists, occupied):
    coeff_blocks = occupied.reshape(NB, BLK, OCC)

    def advance(running, inputs):
        integrals, listed = inputs
        chosen = jnp.take(coeff_blocks, listed.astype(jnp.int32), axis=0).astype(jnp.float32)
        transformed = jnp.einsum('mnapq,nqi->ampi', integrals.astype(jnp.float32), chosen).astype(jnp.bfloat16)
        transformed = lax.optimization_barrier(transformed)
        widened = transformed.astype(jnp.float32)
        product = jnp.einsum('ampi,anqi->mnpq', widened, widened)
        row_index = jnp.broadcast_to(listed[:, None], (SB, SB)).reshape(-1).astype(jnp.int32)
        offset_index = (listed[None, :] - listed[:, None] + SB).reshape(-1).astype(jnp.int32)
        pieces = product.reshape(SB * SB, BLK, BLK)
        return running.at[row_index, :, offset_index, :].add(pieces), None

    zeroed = jnp.zeros((NB, BLK, BAND, BLK), jnp.float32)
    running, unused = lax.scan(advance, zeroed, (three_centre, block_lists))
    return running.reshape(NB, BLK, BAND * BLK)
```

```python
import functools

import jax
import jax.numpy as jnp
from jax import lax
from jax.experimental import pallas as pl
from jax.experimental.pallas import tpu as pltpu
from jax.sharding import PartitionSpec as P

ROWS_BY_ROWS = (((1,), (1,)), ((), ()))


def contract_rows(left, right):
    return lax.dot_general(left, right, ROWS_BY_ROWS, preferred_element_type=jnp.float32)


def band_kernel(sizes, place_ref, lists_ref, *refs):
    aux_blocks, span, depth, edge, width, slots, groups = sizes
    coeff_refs, refs = refs[:slots], refs[slots:]
    integrals_ref, keep_ref, send_ref = refs[:3]
    coeffs, chosen, integrals, half, total, band, load_sem, coeff_sem, out_sem = refs[3:]
    orb, aux = place_ref[0], place_ref[1]
    rows = edge // groups

    def load(block, m):
        return pltpu.make_async_copy(integrals_ref.at[block, m], integrals.at[m], load_sem.at[m])

    coeff_loads = [pltpu.make_async_copy(coeff_refs[s], coeffs.at[s], coeff_sem.at[s]) for s in range(slots)]
    for copy in coeff_loads:
        copy.start()
    for m in range(span):
        load(0, m).start()
    band[...] = jnp.zeros_like(band)
    for copy in coeff_loads:
        copy.wait()

    def step(block, carry):
        listed = [lists_ref[block, j] for j in range(span)]
        for n in range(span):
            chosen[n * edge : (n + 1) * edge, :] = coeffs[listed[n] ^ orb]
        for m in range(span):
            load(block, m).wait()
            left = jnp.concatenate([integrals[m, n].reshape(depth * edge, edge) for n in range(span)], axis=1)
            made = jnp.dot(left, chosen[...], preferred_element_type=jnp.float32).astype(jnp.bfloat16)
            for a in range(depth):
                half[m * edge : (m + 1) * edge, a * width : (a + 1) * width] = made[a * edge : (a + 1) * edge]

            @pl.when(block + 1 < aux_blocks)
            def _():
                load(block + 1, m).start()

        last = (span - 1) * edge
        total[:, :last] = contract_rows(half[...], half[:last])
        total[last:, last:] = contract_rows(half[last:], half[last:])
        for m in range(span):
            for n in range(m + 1):
                piece = total[m * edge : (m + 1) * edge, n * edge : (n + 1) * edge]
                pairs = [(m, n, piece)] if m == n else [(m, n, piece), (n, m, piece.T)]
                for j, k, value in pairs:
                    slot = listed[j] ^ orb
                    offset = listed[k] - listed[j] + span
                    for g in range(groups):
                        place = (slot & 1, slot >> 1, g ^ aux, offset)
                        band[place] += value[g * rows : (g + 1) * rows]
        return carry

    lax.fori_loop(0, aux_blocks, step, 0)
    outs = [pltpu.make_async_copy(band.at[i], ref, out_sem.at[i]) for i, ref in enumerate((keep_ref, send_ref))]
    for copy in outs:
        copy.start()
    for copy in outs:
        copy.wait()


def band_partials(place, block_lists, coeff_slots, three_centre, groups):
    aux_blocks, span, _, depth, edge, _ = three_centre.shape
    width = coeff_slots[0].shape[1]
    slots = len(coeff_slots)
    offsets = 2 * span + 1
    sizes = (aux_blocks, span, depth, edge, width, slots, groups)
    part = (slots // 2, groups, offsets, edge // groups, edge)
    anywhere = pl.BlockSpec(memory_space=pl.ANY)
    scalars = pl.BlockSpec(memory_space=pltpu.SMEM)
    return pl.pallas_call(
        functools.partial(band_kernel, sizes),
        out_shape=[jax.ShapeDtypeStruct(part, jnp.float32)] * 2,
        in_specs=[scalars, scalars] + [anywhere] * (slots + 1),
        out_specs=[anywhere] * 2,
        scratch_shapes=[
            pltpu.VMEM((slots, edge, width), jnp.bfloat16),
            pltpu.VMEM((span * edge, width), jnp.bfloat16),
            pltpu.VMEM((span, span, depth, edge, edge), jnp.bfloat16),
            pltpu.VMEM((span * edge, depth * width), jnp.bfloat16),
            pltpu.VMEM((span * edge, span * edge), jnp.float32),
            pltpu.VMEM((2,) + part, jnp.float32),
            pltpu.SemaphoreType.DMA((span,)),
            pltpu.SemaphoreType.DMA((slots,)),
            pltpu.SemaphoreType.DMA((2,)),
        ],
        compiler_params=pltpu.CompilerParams(vmem_limit_bytes=56 * 2**20),
        name="band_partials",
    )(place, block_lists, *coeff_slots, three_centre)


def per_device(orb_size, aux_size, three_centre, block_lists, occupied):
    def swap(value, axis, bits):
        size = {"orb": orb_size, "aux": aux_size}[axis]
        return lax.ppermute(value, axis, [(i, i ^ bits) for i in range(size)])

    place = jnp.stack([lax.axis_index("orb"), lax.axis_index("aux")]).astype(jnp.int32)
    slots = {0: occupied, 1: swap(occupied, "orb", 1)}
    for s in range(2, orb_size, 2):
        slots[s] = swap(occupied, "orb", s)
    for s in range(2, orb_size, 2):
        slots[s + 1] = swap(slots[s], "orb", 1)
    keep, send = band_partials(place, block_lists, [slots[s] for s in range(orb_size)], three_centre, aux_size)

    summed = keep + swap(send, "orb", 1)
    bits = list(range(1, orb_size.bit_length() - 1))
    halves = []
    for part in range(2):
        taken = summed[:, part * (aux_size // 2) : (part + 1) * (aux_size // 2)]
        taken = taken.reshape((2,) * len(bits) + taken.shape[1:])
        left = bits[::-1]
        for bit in bits if part == 0 else left[:]:
            axis = left.index(bit)
            kept = lax.index_in_dim(taken, 0, axis, keepdims=False)
            taken = kept + swap(lax.index_in_dim(taken, 1, axis, keepdims=False), "orb", 1 << bit)
            left.remove(bit)
        halves.append(taken)
    rows = jnp.concatenate(halves, axis=0)
    step = 1
    while step < aux_size:
        rows = rows[0::2] + swap(rows[1::2], "aux", step)
        step *= 2
    return jnp.transpose(rows, (0, 2, 1, 3)).reshape(1, rows.shape[2], rows.shape[1] * rows.shape[3])


def solution(mesh):
    return jax.shard_map(
        functools.partial(per_device, mesh.shape["orb"], mesh.shape["aux"]),
        mesh=mesh,
        in_specs=(
            P(("aux", "orb"), None, None, None, None, None),
            P(("aux", "orb"), None),
            P("orb", None),
        ),
        out_specs=P("orb", "aux", None),
        check_vma=False,
    )
```

```python
import functools

import jax
import jax.numpy as jnp
from jax import lax
from jax.experimental import pallas as pl
from jax.experimental.pallas import tpu as pltpu
from jax.sharding import PartitionSpec as P


def band_kernel(sizes, place_ref, lists_ref, *refs):
    aux_blocks, span, depth, edge, width, slots, groups = sizes
    coeff_refs, refs = refs[:slots], refs[slots:]
    integrals_ref, keep_ref, send_ref = refs[:3]
    coeffs, chosen, integrals, half, flipped, total, band, load_sem, coeff_sem, out_sem = refs[3:]
    orb, aux = place_ref[0], place_ref[1]
    rows = edge // groups

    def load(block, m):
        into = integrals.at[block % 2, m]
        return pltpu.make_async_copy(integrals_ref.at[block, m], into, load_sem.at[block % 2, m])

    for m in range(span):
        load(0, m).start()
    coeff_loads = [pltpu.make_async_copy(coeff_refs[s], coeffs.at[s], coeff_sem.at[s]) for s in range(slots)]
    for copy in coeff_loads:
        copy.start()
    band[...] = jnp.zeros_like(band)
    for copy in coeff_loads:
        copy.wait()

    def step(block, carry):
        @pl.when(block + 1 < aux_blocks)
        def _():
            for m in range(span):
                load(block + 1, m).start()

        listed = [lists_ref[block, j] for j in range(span)]
        for n in range(span):
            chosen[n * edge : (n + 1) * edge, :] = coeffs[listed[n] ^ orb]
        for m in range(span):
            load(block, m).wait()
        for m in range(span):
            pieces = [integrals[block % 2, m, n].reshape(depth * edge, edge) for n in range(span)]
            left = jnp.concatenate(pieces, axis=1)
            made = jnp.dot(left, chosen[...], preferred_element_type=jnp.float32).astype(jnp.bfloat16)
            for a in range(depth):
                piece = made[a * edge : (a + 1) * edge]
                half[m * edge : (m + 1) * edge, a * width : (a + 1) * width] = piece
                flipped[a * width : (a + 1) * width, m * edge : (m + 1) * edge] = piece.T

        for i in range(span):
            columns = [flipped[:, j * edge : (j + 1) * edge] for j in (i, (i + 1) % span)]
            made = jnp.dot(
                half[i * edge : (i + 1) * edge],
                jnp.concatenate(columns, axis=1),
                preferred_element_type=jnp.float32,
            )
            here = slice(i * edge, (i + 1) * edge)
            total[here, here] = made[:, :edge]
            if i + 1 < span:
                total[here, (i + 1) * edge : (i + 2) * edge] = made[:, edge:]
            else:
                total[:edge, here] = made[:, edge:].T
        for j in range(span):
            for k in range(j, span):
                place = (listed[j] ^ orb, listed[k] - listed[j] + span)
                band[place] += total[j * edge : (j + 1) * edge, k * edge : (k + 1) * edge]
        return carry

    lax.fori_loop(0, aux_blocks, step, 0)

    for slot in range(slots):
        for offset in range(1, span + 1):
            row = slot ^ orb

            @pl.when(row + offset < slots)
            def _():
                band[(row + offset) ^ orb, span - offset] = band[slot, span + offset].T

    outs = []
    for side, ref in enumerate((keep_ref, send_ref)):
        for s in range(slots // 2):
            for g in range(groups):
                source = band.at[2 * s + side, :, pl.ds(g * rows, rows)]
                outs.append(pltpu.make_async_copy(source, ref.at[s, g ^ aux], out_sem.at[side, s, g]))
    for copy in outs:
        copy.start()
    for copy in outs:
        copy.wait()


def band_partials(place, block_lists, coeff_slots, three_centre, groups):
    aux_blocks, span, _, depth, edge, _ = three_centre.shape
    width = coeff_slots[0].shape[1]
    slots = len(coeff_slots)
    offsets = 2 * span + 1
    sizes = (aux_blocks, span, depth, edge, width, slots, groups)
    part = (slots // 2, groups, offsets, edge // groups, edge)
    anywhere = pl.BlockSpec(memory_space=pl.ANY)
    scalars = pl.BlockSpec(memory_space=pltpu.SMEM)
    return pl.pallas_call(
        functools.partial(band_kernel, sizes),
        out_shape=[jax.ShapeDtypeStruct(part, jnp.float32)] * 2,
        in_specs=[scalars, scalars] + [anywhere] * (slots + 1),
        out_specs=[anywhere] * 2,
        scratch_shapes=[
            pltpu.VMEM((slots, edge, width), jnp.bfloat16),
            pltpu.VMEM((span * edge, width), jnp.bfloat16),
            pltpu.VMEM((2, span, span, depth, edge, edge), jnp.bfloat16),
            pltpu.VMEM((span * edge, depth * width), jnp.bfloat16),
            pltpu.VMEM((depth * width, span * edge), jnp.bfloat16),
            pltpu.VMEM((span * edge, span * edge), jnp.float32),
            pltpu.VMEM((slots, offsets, edge, edge), jnp.float32),
            pltpu.SemaphoreType.DMA((2, span)),
            pltpu.SemaphoreType.DMA((slots,)),
            pltpu.SemaphoreType.DMA((2, slots // 2, groups)),
        ],
        compiler_params=pltpu.CompilerParams(vmem_limit_bytes=56 * 2**20),
        name="band_partials",
    )(place, block_lists, *coeff_slots, three_centre)


def per_device(orb_size, aux_size, three_centre, block_lists, occupied):
    def swap(value, axis, bits):
        size = {"orb": orb_size, "aux": aux_size}[axis]
        return lax.ppermute(value, axis, [(i, i ^ bits) for i in range(size)])

    place = jnp.stack([lax.axis_index("orb"), lax.axis_index("aux")]).astype(jnp.int32)
    slots = {0: occupied, 1: swap(occupied, "orb", 1)}
    for s in range(2, orb_size, 2):
        slots[s] = swap(occupied, "orb", s)
    for s in range(2, orb_size, 2):
        slots[s + 1] = swap(slots[s], "orb", 1)
    keep, send = band_partials(place, block_lists, [slots[s] for s in range(orb_size)], three_centre, aux_size)

    summed = keep + swap(send, "orb", 1)
    bits = list(range(1, orb_size.bit_length() - 1))
    halves = []
    for part in range(2):
        taken = summed[:, part * (aux_size // 2) : (part + 1) * (aux_size // 2)]
        taken = taken.reshape((2,) * len(bits) + taken.shape[1:])
        left = bits[::-1]
        for bit in bits if part == 0 else left[:]:
            axis = left.index(bit)
            kept = lax.index_in_dim(taken, 0, axis, keepdims=False)
            taken = kept + swap(lax.index_in_dim(taken, 1, axis, keepdims=False), "orb", 1 << bit)
            left.remove(bit)
        halves.append(taken)
    rows = jnp.concatenate(halves, axis=0)
    step = 1
    while step < aux_size:
        rows = rows[0::2] + swap(rows[1::2], "aux", step)
        step *= 2
    return jnp.transpose(rows, (0, 2, 1, 3)).reshape(1, rows.shape[2], rows.shape[1] * rows.shape[3])


def solution(mesh):
    return jax.shard_map(
        functools.partial(per_device, mesh.shape["orb"], mesh.shape["aux"]),
        mesh=mesh,
        in_specs=(
            P(("aux", "orb"), None, None, None, None, None),
            P(("aux", "orb"), None),
            P("orb", None),
        ),
        out_specs=P("orb", "aux", None),
        check_vma=False,
    )
```

```python
import functools
import math

import jax
import jax.numpy as jnp
from jax import lax
from jax.experimental import pallas as pl
from jax.experimental.pallas import tpu as pltpu
from jax.sharding import PartitionSpec as P


def band_kernel(sizes, lists_ref, *refs):
    aux_blocks, span, depth, edge, width, slots, groups = sizes
    coeff_refs, refs = refs[:slots], refs[slots:]
    integrals_ref, keep_ref, send_ref = refs[:3]
    coeffs, chosen, integrals, half, flipped, total, band, load_sem, coeff_sem, out_sem = refs[3:]
    orb, aux = lax.axis_index("orb"), lax.axis_index("aux")
    rows = edge // groups

    def load(block, m):
        into = integrals.at[block % 2, m]
        return pltpu.make_async_copy(integrals_ref.at[block, m], into, load_sem.at[block % 2, m])

    for m in range(span):
        load(0, m).start()
    coeff_loads = [pltpu.make_async_copy(coeff_refs[s], coeffs.at[s], coeff_sem.at[s]) for s in range(slots)]
    for copy in coeff_loads:
        copy.start()
    band[...] = jnp.zeros_like(band)
    for copy in coeff_loads:
        copy.wait()

    def step(block, carry):
        @pl.when(block + 1 < aux_blocks)
        def _():
            for m in range(span):
                load(block + 1, m).start()

        listed = [lists_ref[block, j] for j in range(span)]
        for n in range(span):
            chosen[n * edge : (n + 1) * edge, :] = coeffs[listed[n] ^ orb]
        for m in range(span):
            load(block, m).wait()
        for m in range(span):
            pieces = [integrals[block % 2, m, n].reshape(depth * edge, edge) for n in range(span)]
            left = jnp.concatenate(pieces, axis=1)
            made = jnp.dot(left, chosen[...], preferred_element_type=jnp.float32).astype(jnp.bfloat16)
            for a in range(depth):
                piece = made[a * edge : (a + 1) * edge]
                half[m * edge : (m + 1) * edge, a * width : (a + 1) * width] = piece
                flipped[a * width : (a + 1) * width, m * edge : (m + 1) * edge] = piece.T

        for i in range(span):
            columns = [flipped[:, j * edge : (j + 1) * edge] for j in (i, (i + 1) % span)]
            made = jnp.dot(
                half[i * edge : (i + 1) * edge],
                jnp.concatenate(columns, axis=1),
                preferred_element_type=jnp.float32,
            )
            here = slice(i * edge, (i + 1) * edge)
            total[here, here] = made[:, :edge]
            if i + 1 < span:
                total[here, (i + 1) * edge : (i + 2) * edge] = made[:, edge:]
            else:
                total[:edge, here] = made[:, edge:].T
        for j in range(span):
            for k in range(j, span):
                place = (listed[j] ^ orb, listed[k] - listed[j] + span)
                band[place] += total[j * edge : (j + 1) * edge, k * edge : (k + 1) * edge]
        return carry

    lax.fori_loop(0, aux_blocks, step, 0)

    for slot in range(slots):
        for offset in range(1, span + 1):
            row = slot ^ orb

            @pl.when(row + offset < slots)
            def _():
                band[(row + offset) ^ orb, span - offset] = band[slot, span + offset].T

    outs = []
    for side, ref in enumerate((keep_ref, send_ref)):
        for s in range(slots // 2):
            for g in range(groups):
                source = band.at[2 * s + side, :, pl.ds(g * rows, rows)]
                outs.append(pltpu.make_async_copy(source, ref.at[s, g ^ aux], out_sem.at[side, s, g]))
    for copy in outs:
        copy.start()
    for copy in outs:
        copy.wait()


def band_partials(block_lists, coeff_slots, three_centre, groups):
    aux_blocks, span, _, depth, edge, _ = three_centre.shape
    width = coeff_slots[0].shape[1]
    slots = len(coeff_slots)
    offsets = 2 * span + 1
    sizes = (aux_blocks, span, depth, edge, width, slots, groups)
    part = (slots // 2, groups, offsets, edge // groups, edge)
    anywhere = pl.BlockSpec(memory_space=pl.ANY)
    scalars = pl.BlockSpec(memory_space=pltpu.SMEM)
    buffers = [
        pltpu.VMEM((slots, edge, width), jnp.bfloat16),
        pltpu.VMEM((span * edge, width), jnp.bfloat16),
        pltpu.VMEM((2, span, span, depth, edge, edge), jnp.bfloat16),
        pltpu.VMEM((span * edge, depth * width), jnp.bfloat16),
        pltpu.VMEM((depth * width, span * edge), jnp.bfloat16),
        pltpu.VMEM((span * edge, span * edge), jnp.float32),
        pltpu.VMEM((slots, offsets, edge, edge), jnp.float32),
    ]
    held = sum(math.prod(b.shape) * jnp.dtype(b.dtype).itemsize for b in buffers)
    return pl.pallas_call(
        functools.partial(band_kernel, sizes),
        out_shape=[jax.ShapeDtypeStruct(part, jnp.float32)] * 2,
        in_specs=[scalars] + [anywhere] * (slots + 1),
        out_specs=[anywhere] * 2,
        scratch_shapes=buffers
        + [
            pltpu.SemaphoreType.DMA((2, span)),
            pltpu.SemaphoreType.DMA((slots,)),
            pltpu.SemaphoreType.DMA((2, slots // 2, groups)),
        ],
        compiler_params=pltpu.CompilerParams(vmem_limit_bytes=held + 8 * 2**20),
        name="band_partials",
    )(block_lists, *coeff_slots, three_centre)


LEVELS = 32767
STEPS = 64
LIFT = 30
FLOOR = -100


def encode(value):
    lead, (offsets, rows, lanes) = value.shape[:-3], value.shape[-3:]
    lifted = value * 2.0**LIFT
    top = jnp.max(jnp.abs(lifted), axis=-2, keepdims=True)
    exponent = jnp.log2(jnp.maximum(top, 2.0 ** (FLOOR + 15))) - 15.0
    exponent = jnp.floor(exponent * STEPS) + 2.0
    scaled = lifted * jnp.exp2(exponent * (-1.0 / STEPS))
    coded = jnp.clip(jnp.round(scaled), -LEVELS, LEVELS).astype(jnp.int16)
    coded = coded.reshape(lead + (offsets * rows, lanes))
    scales = exponent.astype(jnp.int16).reshape(lead + (offsets, lanes))
    blank = jnp.zeros(lead + (-offsets % 16, lanes), jnp.int16)
    return jnp.concatenate([coded, scales, blank], axis=-2)


def decode(coded, offsets, rows):
    lead, lanes = coded.shape[:-2], coded.shape[-1]
    values = coded[..., : offsets * rows, :].reshape(lead + (offsets, rows, lanes)).astype(jnp.float32)
    exponent = coded[..., offsets * rows : offsets * (rows + 1), :].astype(jnp.float32)
    scale = jnp.exp2(exponent * (1.0 / STEPS)) * 2.0**-LIFT
    return values * scale.reshape(lead + (offsets, 1, lanes))


def per_device(orb_size, aux_size, three_centre, block_lists, occupied):
    def swap(value, axis, bits):
        size = {"orb": orb_size, "aux": aux_size}[axis]
        return lax.ppermute(value, axis, [(i, i ^ bits) for i in range(size)])

    def swap_sums(value, axis, bits):
        return decode(swap(encode(value), axis, bits), *value.shape[-3:-1])

    slots = {0: occupied, 1: swap(occupied, "orb", 1)}
    for s in range(2, orb_size, 2):
        slots[s] = swap(occupied, "orb", s)
    arrived, block_lists = lax.optimization_barrier(([slots[s] for s in range(2, orb_size, 2)], block_lists + 0))
    for s in range(2, orb_size, 2):
        slots[s] = arrived[s // 2 - 1]
        slots[s + 1] = swap(slots[s], "orb", 1)
    keep, send = band_partials(block_lists, [slots[s] for s in range(orb_size)], three_centre, aux_size)

    summed = keep + swap(send, "orb", 1)
    bits = list(range(1, orb_size.bit_length() - 1))
    halves = []
    for part in range(2):
        taken = summed[:, part * (aux_size // 2) : (part + 1) * (aux_size // 2)]
        taken = taken.reshape((2,) * len(bits) + taken.shape[1:])
        left = bits[::-1]
        for bit in bits if part == 0 else left[:]:
            axis = left.index(bit)
            kept = lax.index_in_dim(taken, 0, axis, keepdims=False)
            taken = kept + swap_sums(lax.index_in_dim(taken, 1, axis, keepdims=False), "orb", 1 << bit)
            left.remove(bit)
        halves.append(taken)
    rows = jnp.concatenate(halves, axis=0)
    step = 1
    while step < aux_size:
        rows = rows[0::2] + swap_sums(rows[1::2], "aux", step)
        step *= 2
    return jnp.transpose(rows, (0, 2, 1, 3)).reshape(1, rows.shape[2], rows.shape[1] * rows.shape[3])


def solution(mesh):
    return jax.shard_map(
        functools.partial(per_device, mesh.shape["orb"], mesh.shape["aux"]),
        mesh=mesh,
        in_specs=(
            P(("aux", "orb"), None, None, None, None, None),
            P(("aux", "orb"), None),
            P("orb", None),
        ),
        out_specs=P("orb", "aux", None),
        check_vma=False,
    )
```

```python
import functools
import math

import jax
import jax.numpy as jnp
from jax import lax
from jax.experimental import pallas as pl
from jax.experimental.pallas import tpu as pltpu
from jax.sharding import PartitionSpec as P


def band_kernel(sizes, lists_ref, *refs):
    aux_blocks, span, depth, edge, width, slots, groups = sizes
    coeff_refs, refs = refs[:slots], refs[slots:]
    integrals_ref, keep_ref, send_ref = refs[:3]
    coeffs, chosen, integrals, half, flipped, total, band, load_sem, coeff_sem, out_sem = refs[3:]
    orb, aux = lax.axis_index("orb"), lax.axis_index("aux")
    rows = edge // groups

    def load(block, m):
        into = integrals.at[block % 2, m]
        return pltpu.make_async_copy(integrals_ref.at[block, m], into, load_sem.at[block % 2, m])

    for m in range(span):
        load(0, m).start()
    coeff_loads = [pltpu.make_async_copy(coeff_refs[s], coeffs.at[s], coeff_sem.at[s]) for s in range(slots)]
    for copy in coeff_loads:
        copy.start()
    band[...] = jnp.zeros_like(band)
    for copy in coeff_loads:
        copy.wait()

    def step(block, carry):
        @pl.when(block + 1 < aux_blocks)
        def _():
            for m in range(span):
                load(block + 1, m).start()

        listed = [lists_ref[block, j] for j in range(span)]
        for n in range(span):
            chosen[n * edge : (n + 1) * edge, :] = coeffs[listed[n] ^ orb]
        for m in range(span):
            load(block, m).wait()
        for m in range(span):
            pieces = [integrals[block % 2, m, n].reshape(depth * edge, edge) for n in range(span)]
            left = jnp.concatenate(pieces, axis=1)
            made = jnp.dot(left, chosen[...], preferred_element_type=jnp.float32).astype(jnp.bfloat16)
            for a in range(depth):
                piece = made[a * edge : (a + 1) * edge]
                half[m * edge : (m + 1) * edge, a * width : (a + 1) * width] = piece
                flipped[a * width : (a + 1) * width, m * edge : (m + 1) * edge] = piece.T

        for i in range(span):
            columns = [flipped[:, j * edge : (j + 1) * edge] for j in (i, (i + 1) % span)]
            made = jnp.dot(
                half[i * edge : (i + 1) * edge],
                jnp.concatenate(columns, axis=1),
                preferred_element_type=jnp.float32,
            )
            here = slice(i * edge, (i + 1) * edge)
            total[here, here] = made[:, :edge]
            if i + 1 < span:
                total[here, (i + 1) * edge : (i + 2) * edge] = made[:, edge:]
            else:
                total[:edge, here] = made[:, edge:].T
        for j in range(span):
            for k in range(j, span):
                place = (listed[j] ^ orb, listed[k] - listed[j] + span)
                band[place] += total[j * edge : (j + 1) * edge, k * edge : (k + 1) * edge]
        return carry

    lax.fori_loop(0, aux_blocks, step, 0)

    for slot in range(slots):
        for offset in range(1, span + 1):
            row = slot ^ orb

            @pl.when(row + offset < slots)
            def _():
                band[(row + offset) ^ orb, span - offset] = band[slot, span + offset].T

    outs = []
    for side, ref in enumerate((keep_ref, send_ref)):
        for s in range(slots // 2):
            for g in range(groups):
                source = band.at[2 * s + side, :, pl.ds(g * rows, rows)]
                outs.append(pltpu.make_async_copy(source, ref.at[s, g ^ aux], out_sem.at[side, s, g]))
    for copy in outs:
        copy.start()
    for copy in outs:
        copy.wait()


def band_partials(block_lists, coeff_slots, three_centre, groups):
    aux_blocks, span, _, depth, edge, _ = three_centre.shape
    width = coeff_slots[0].shape[1]
    slots = len(coeff_slots)
    offsets = 2 * span + 1
    sizes = (aux_blocks, span, depth, edge, width, slots, groups)
    part = (slots // 2, groups, offsets, edge // groups, edge)
    anywhere = pl.BlockSpec(memory_space=pl.ANY)
    in_place = pl.BlockSpec(memory_space=pltpu.HBM)
    scalars = pl.BlockSpec(memory_space=pltpu.SMEM)
    buffers = [
        pltpu.VMEM((slots, edge, width), jnp.bfloat16),
        pltpu.VMEM((span * edge, width), jnp.bfloat16),
        pltpu.VMEM((2, span, span, depth, edge, edge), jnp.bfloat16),
        pltpu.VMEM((span * edge, depth * width), jnp.bfloat16),
        pltpu.VMEM((depth * width, span * edge), jnp.bfloat16),
        pltpu.VMEM((span * edge, span * edge), jnp.float32),
        pltpu.VMEM((slots, offsets, edge, edge), jnp.float32),
    ]
    held = sum(math.prod(b.shape) * jnp.dtype(b.dtype).itemsize for b in buffers)
    return pl.pallas_call(
        functools.partial(band_kernel, sizes),
        out_shape=[jax.ShapeDtypeStruct(part, jnp.float32)] * 2,
        in_specs=[scalars, in_place] + [anywhere] * (slots - 1) + [in_place],
        out_specs=[anywhere] * 2,
        scratch_shapes=buffers
        + [
            pltpu.SemaphoreType.DMA((2, span)),
            pltpu.SemaphoreType.DMA((slots,)),
            pltpu.SemaphoreType.DMA((2, slots // 2, groups)),
        ],
        compiler_params=pltpu.CompilerParams(vmem_limit_bytes=held + 8 * 2**20),
        name="band_partials",
    )(block_lists, *coeff_slots, three_centre)


LEVELS = 32767
STEPS = 64
LIFT = 30
FLOOR = -100


def encode(value):
    lead, (offsets, rows, lanes) = value.shape[:-3], value.shape[-3:]
    lifted = value * 2.0**LIFT
    top = jnp.max(jnp.abs(lifted), axis=-2, keepdims=True)
    exponent = jnp.log2(jnp.maximum(top, 2.0 ** (FLOOR + 15))) - 15.0
    exponent = jnp.floor(exponent * STEPS) + 2.0
    scaled = lifted * jnp.exp2(exponent * (-1.0 / STEPS))
    coded = jnp.clip(jnp.round(scaled), -LEVELS, LEVELS).astype(jnp.int16)
    coded = coded.reshape(lead + (offsets * rows, lanes))
    scales = exponent.astype(jnp.int16).reshape(lead + (offsets, lanes))
    blank = jnp.zeros(lead + (-offsets % 16, lanes), jnp.int16)
    return jnp.concatenate([coded, scales, blank], axis=-2)


def decode(coded, offsets, rows):
    lead, lanes = coded.shape[:-2], coded.shape[-1]
    values = coded[..., : offsets * rows, :].reshape(lead + (offsets, rows, lanes)).astype(jnp.float32)
    exponent = coded[..., offsets * rows : offsets * (rows + 1), :].astype(jnp.float32)
    scale = jnp.exp2(exponent * (1.0 / STEPS)) * 2.0**-LIFT
    return values * scale.reshape(lead + (offsets, 1, lanes))


def per_device(orb_size, aux_size, three_centre, block_lists, occupied):
    def swap(value, axis, bits):
        size = {"orb": orb_size, "aux": aux_size}[axis]
        return lax.ppermute(value, axis, [(i, i ^ bits) for i in range(size)])

    def swap_sums(value, axis, bits):
        return decode(swap(encode(value), axis, bits), *value.shape[-3:-1])

    slots = {0: occupied, 1: swap(occupied, "orb", 1)}
    for s in range(2, orb_size, 2):
        slots[s] = swap(occupied, "orb", s)
    slots[2], block_lists = lax.optimization_barrier((slots[2], block_lists + 0))
    for s in range(2, orb_size, 2):
        slots[s + 1] = swap(slots[s], "orb", 1)
    keep, send = band_partials(block_lists, [slots[s] for s in range(orb_size)], three_centre, aux_size)

    summed = keep + swap(send, "orb", 1)
    bits = list(range(1, orb_size.bit_length() - 1))
    halves = []
    for part in range(2):
        taken = summed[:, part * (aux_size // 2) : (part + 1) * (aux_size // 2)]
        taken = taken.reshape((2,) * len(bits) + taken.shape[1:])
        left = bits[::-1]
        for bit in bits if part == 0 else left[:]:
            axis = left.index(bit)
            kept = lax.index_in_dim(taken, 0, axis, keepdims=False)
            taken = kept + swap_sums(lax.index_in_dim(taken, 1, axis, keepdims=False), "orb", 1 << bit)
            left.remove(bit)
        halves.append(taken)
    rows = jnp.concatenate(halves, axis=0)
    rows = sum((swap_sums(rows[g : g + 1], "aux", g) for g in range(1, aux_size)), rows[:1])
    return jnp.transpose(rows, (0, 2, 1, 3)).reshape(1, rows.shape[2], rows.shape[1] * rows.shape[3])


def solution(mesh):
    return jax.shard_map(
        functools.partial(per_device, mesh.shape["orb"], mesh.shape["aux"]),
        mesh=mesh,
        in_specs=(
            P(("aux", "orb"), None, None, None, None, None),
            P(("aux", "orb"), None),
            P("orb", None),
        ),
        out_specs=P("orb", "aux", None),
        check_vma=False,
    )
```

```python
import functools
import math

import jax
import jax.numpy as jnp
from jax import lax
from jax.experimental import pallas as pl
from jax.experimental.pallas import tpu as pltpu
from jax.sharding import PartitionSpec as P


def band_kernel(sizes, lists_ref, *refs):
    aux_blocks, span, depth, edge, width, slots, groups = sizes
    coeff_refs, refs = refs[:slots], refs[slots:]
    integrals_ref, keep_ref, send_ref = refs[:3]
    coeffs, chosen, integrals, half, flipped, total, band, load_sem, coeff_sem = refs[3:]
    orb, aux = lax.axis_index("orb"), lax.axis_index("aux")
    rows = edge // groups

    def load(block, m):
        into = integrals.at[block % 2, m]
        return pltpu.make_async_copy(integrals_ref.at[block, m], into, load_sem.at[block % 2, m])

    for m in range(span):
        load(0, m).start()
    coeff_loads = [pltpu.make_async_copy(coeff_refs[s], coeffs.at[s], coeff_sem.at[s]) for s in range(slots)]
    for copy in coeff_loads:
        copy.start()
    band[...] = jnp.zeros_like(band)
    for copy in coeff_loads:
        copy.wait()

    def step(block, carry):
        @pl.when(block + 1 < aux_blocks)
        def _():
            for m in range(span):
                load(block + 1, m).start()

        listed = [lists_ref[block, j] for j in range(span)]
        for n in range(span):
            chosen[n * edge : (n + 1) * edge, :] = coeffs[listed[n] ^ orb]
        for m in range(span):
            load(block, m).wait()
        for m in range(span):
            pieces = [integrals[block % 2, m, n].reshape(depth * edge, edge) for n in range(span)]
            left = jnp.concatenate(pieces, axis=1)
            made = jnp.dot(left, chosen[...], preferred_element_type=jnp.float32).astype(jnp.bfloat16)
            for a in range(depth):
                piece = made[a * edge : (a + 1) * edge]
                half[m * edge : (m + 1) * edge, a * width : (a + 1) * width] = piece
                flipped[a * width : (a + 1) * width, m * edge : (m + 1) * edge] = piece.T

        for i in range(span):
            columns = [flipped[:, j * edge : (j + 1) * edge] for j in (i, (i + 1) % span)]
            made = jnp.dot(
                half[i * edge : (i + 1) * edge],
                jnp.concatenate(columns, axis=1),
                preferred_element_type=jnp.float32,
            )
            here = slice(i * edge, (i + 1) * edge)
            total[here, here] = made[:, :edge]
            if i + 1 < span:
                total[here, (i + 1) * edge : (i + 2) * edge] = made[:, edge:]
            else:
                total[:edge, here] = made[:, edge:].T
        for j in range(span):
            for k in range(j, span):
                place = (listed[j] ^ orb, listed[k] - listed[j] + span)
                band[place] += total[j * edge : (j + 1) * edge, k * edge : (k + 1) * edge]
        return carry

    lax.fori_loop(0, aux_blocks, step, 0)

    for slot in range(slots):
        for offset in range(1, span + 1):
            row = slot ^ orb

            @pl.when(row + offset < slots)
            def _():
                band[(row + offset) ^ orb, span - offset] = band[slot, span + offset].T

    for side, ref in enumerate((keep_ref, send_ref)):
        for s in range(slots // 2):
            for g in range(groups):
                ref[s, g ^ aux] = band[2 * s + side, :, g * rows : (g + 1) * rows]


def band_partials(block_lists, coeff_slots, three_centre, groups):
    aux_blocks, span, _, depth, edge, _ = three_centre.shape
    width = coeff_slots[0].shape[1]
    slots = len(coeff_slots)
    offsets = 2 * span + 1
    sizes = (aux_blocks, span, depth, edge, width, slots, groups)
    part = (slots // 2, groups, offsets, edge // groups, edge)
    anywhere = pl.BlockSpec(memory_space=pl.ANY)
    scalars = pl.BlockSpec(memory_space=pltpu.SMEM)
    buffers = [
        pltpu.VMEM((slots, edge, width), jnp.bfloat16),
        pltpu.VMEM((span * edge, width), jnp.bfloat16),
        pltpu.VMEM((2, span, span, depth, edge, edge), jnp.bfloat16),
        pltpu.VMEM((span * edge, depth * width), jnp.bfloat16),
        pltpu.VMEM((depth * width, span * edge), jnp.bfloat16),
        pltpu.VMEM((span * edge, span * edge), jnp.float32),
        pltpu.VMEM((slots, offsets, edge, edge), jnp.float32),
    ]
    held = sum(math.prod(b.shape) * jnp.dtype(b.dtype).itemsize for b in buffers)
    given = 2 * math.prod(part) * 4
    return pl.pallas_call(
        functools.partial(band_kernel, sizes),
        out_shape=[jax.ShapeDtypeStruct(part, jnp.float32)] * 2,
        in_specs=[scalars] + [anywhere] * (slots + 1),
        out_specs=[pl.BlockSpec(memory_space=pltpu.VMEM)] * 2,
        scratch_shapes=buffers
        + [
            pltpu.SemaphoreType.DMA((2, span)),
            pltpu.SemaphoreType.DMA((slots,)),
        ],
        compiler_params=pltpu.CompilerParams(vmem_limit_bytes=held + given + 4 * 2**20),
        name="band_partials",
    )(block_lists, *coeff_slots, three_centre)


LEVELS = 32767
STEPS = 64
LIFT = 30
FLOOR = -100


def encode(value):
    lead, (offsets, rows, lanes) = value.shape[:-3], value.shape[-3:]
    lifted = value * 2.0**LIFT
    top = jnp.max(jnp.abs(lifted), axis=-2, keepdims=True)
    exponent = jnp.log2(jnp.maximum(top, 2.0 ** (FLOOR + 15))) - 15.0
    exponent = jnp.floor(exponent * STEPS) + 2.0
    scaled = lifted * jnp.exp2(exponent * (-1.0 / STEPS))
    coded = jnp.clip(jnp.round(scaled), -LEVELS, LEVELS).astype(jnp.int16)
    coded = coded.reshape(lead + (offsets * rows, lanes))
    scales = exponent.astype(jnp.int16).reshape(lead + (offsets, lanes))
    blank = jnp.zeros(lead + (-offsets % 16, lanes), jnp.int16)
    return jnp.concatenate([coded, scales, blank], axis=-2)


def decode(coded, offsets, rows):
    lead, lanes = coded.shape[:-2], coded.shape[-1]
    values = coded[..., : offsets * rows, :].reshape(lead + (offsets, rows, lanes)).astype(jnp.float32)
    exponent = coded[..., offsets * rows : offsets * (rows + 1), :].astype(jnp.float32)
    scale = jnp.exp2(exponent * (1.0 / STEPS)) * 2.0**-LIFT
    return values * scale.reshape(lead + (offsets, 1, lanes))


def per_device(orb_size, aux_size, three_centre, block_lists, occupied):
    def swap(value, axis, bits):
        size = {"orb": orb_size, "aux": aux_size}[axis]
        return lax.ppermute(value, axis, [(i, i ^ bits) for i in range(size)])

    def swap_sums(value, axis, bits):
        return decode(swap(encode(value), axis, bits), *value.shape[-3:-1])

    slots = {0: occupied, 1: swap(occupied, "orb", 1)}
    for s in range(2, orb_size, 2):
        slots[s] = swap(occupied, "orb", s)
    slots[2], block_lists = lax.optimization_barrier((slots[2], block_lists + 0))
    for s in range(2, orb_size, 2):
        slots[s + 1] = swap(slots[s], "orb", 1)
    keep, send = band_partials(block_lists, [slots[s] for s in range(orb_size)], three_centre, aux_size)

    summed = keep + swap(send, "orb", 1)
    bits = list(range(1, orb_size.bit_length() - 1))
    halves = []
    for part in range(2):
        taken = summed[:, part * (aux_size // 2) : (part + 1) * (aux_size // 2)]
        taken = taken.reshape((2,) * len(bits) + taken.shape[1:])
        left = bits[::-1]
        for bit in bits if part == 0 else left[:]:
            axis = left.index(bit)
            kept = lax.index_in_dim(taken, 0, axis, keepdims=False)
            taken = kept + swap_sums(lax.index_in_dim(taken, 1, axis, keepdims=False), "orb", 1 << bit)
            left.remove(bit)
        halves.append(taken)
    rows = jnp.concatenate(halves, axis=0)
    rows = sum((swap_sums(rows[g : g + 1], "aux", g) for g in range(1, aux_size)), rows[:1])
    return jnp.transpose(rows, (0, 2, 1, 3)).reshape(1, rows.shape[2], rows.shape[1] * rows.shape[3])


def solution(mesh):
    return jax.shard_map(
        functools.partial(per_device, mesh.shape["orb"], mesh.shape["aux"]),
        mesh=mesh,
        in_specs=(
            P(("aux", "orb"), None, None, None, None, None),
            P(("aux", "orb"), None),
            P("orb", None),
        ),
        out_specs=P("orb", "aux", None),
        check_vma=False,
    )
```

```python
import functools
import math

import jax
import jax.numpy as jnp
from jax import lax
from jax.experimental import pallas as pl
from jax.experimental.pallas import tpu as pltpu
from jax.sharding import PartitionSpec as P


def band_kernel(sizes, slot_lists_ref, *refs):
    aux_blocks, span, depth, edge, width, slots, groups = sizes
    coeff_refs, refs = refs[:slots], refs[slots:]
    integrals_ref, keep_ref, send_ref = refs[:3]
    coeffs, chosen, integrals, half, flipped, total, band, load_sem, coeff_sem = refs[3:]
    orb, aux = lax.axis_index("orb"), lax.axis_index("aux")
    rows = edge // groups

    def load(block, m):
        into = integrals.at[block % 2, m]
        return pltpu.make_async_copy(integrals_ref.at[block, m], into, load_sem.at[block % 2, m])

    for m in range(span):
        load(0, m).start()
    coeff_loads = [pltpu.make_async_copy(coeff_refs[s], coeffs.at[s], coeff_sem.at[s]) for s in range(slots)]
    for copy in coeff_loads:
        copy.start()
    band[...] = jnp.zeros_like(band)
    for copy in coeff_loads:
        copy.wait()

    def step(block, carry):
        @pl.when(block + 1 < aux_blocks)
        def _():
            for m in range(span):
                load(block + 1, m).start()

        listed = [slot_lists_ref[block, j] ^ orb for j in range(span)]
        for n in range(span):
            chosen[n * edge : (n + 1) * edge, :] = coeffs[listed[n] ^ orb]
        for m in range(span):
            load(block, m).wait()
        for m in range(span):
            pieces = [integrals[block % 2, m, n].reshape(depth * edge, edge) for n in range(span)]
            left = jnp.concatenate(pieces, axis=1)
            made = jnp.dot(left, chosen[...], preferred_element_type=jnp.float32).astype(jnp.bfloat16)
            for a in range(depth):
                piece = made[a * edge : (a + 1) * edge]
                half[m * edge : (m + 1) * edge, a * width : (a + 1) * width] = piece
                flipped[a * width : (a + 1) * width, m * edge : (m + 1) * edge] = piece.T

        for i in range(span):
            columns = [flipped[:, j * edge : (j + 1) * edge] for j in (i, (i + 1) % span)]
            made = jnp.dot(
                half[i * edge : (i + 1) * edge],
                jnp.concatenate(columns, axis=1),
                preferred_element_type=jnp.float32,
            )
            here = slice(i * edge, (i + 1) * edge)
            total[here, here] = made[:, :edge]
            if i + 1 < span:
                total[here, (i + 1) * edge : (i + 2) * edge] = made[:, edge:]
            else:
                total[:edge, here] = made[:, edge:].T
        for j in range(span):
            for k in range(j, span):
                place = (listed[j] ^ orb, listed[k] - listed[j] + span)
                band[place] += total[j * edge : (j + 1) * edge, k * edge : (k + 1) * edge]
        return carry

    lax.fori_loop(0, aux_blocks, step, 0)

    for slot in range(slots):
        for offset in range(1, span + 1):
            row = slot ^ orb

            @pl.when(row + offset < slots)
            def _():
                band[(row + offset) ^ orb, span - offset] = band[slot, span + offset].T

    for side, ref in enumerate((keep_ref, send_ref)):
        for s in range(slots // 2):
            for g in range(groups):
                ref[s, g ^ aux] = band[2 * s + side, :, g * rows : (g + 1) * rows]


def band_partials(slot_lists, coeff_slots, three_centre, groups):
    aux_blocks, span, _, depth, edge, _ = three_centre.shape
    width = coeff_slots[0].shape[1]
    slots = len(coeff_slots)
    offsets = 2 * span + 1
    sizes = (aux_blocks, span, depth, edge, width, slots, groups)
    part = (slots // 2, groups, offsets, edge // groups, edge)
    anywhere = pl.BlockSpec(memory_space=pl.ANY)
    scalars = pl.BlockSpec(memory_space=pltpu.SMEM)
    buffers = [
        pltpu.VMEM((slots, edge, width), jnp.bfloat16),
        pltpu.VMEM((span * edge, width), jnp.bfloat16),
        pltpu.VMEM((2, span, span, depth, edge, edge), jnp.bfloat16),
        pltpu.VMEM((span * edge, depth * width), jnp.bfloat16),
        pltpu.VMEM((depth * width, span * edge), jnp.bfloat16),
        pltpu.VMEM((span * edge, span * edge), jnp.float32),
        pltpu.VMEM((slots, offsets, edge, edge), jnp.float32),
    ]
    held = sum(math.prod(b.shape) * jnp.dtype(b.dtype).itemsize for b in buffers)
    given = 2 * math.prod(part) * 4
    return pl.pallas_call(
        functools.partial(band_kernel, sizes),
        out_shape=[jax.ShapeDtypeStruct(part, jnp.float32)] * 2,
        in_specs=[scalars] + [anywhere] * (slots + 1),
        out_specs=[pl.BlockSpec(memory_space=pltpu.VMEM)] * 2,
        scratch_shapes=buffers
        + [
            pltpu.SemaphoreType.DMA((2, span)),
            pltpu.SemaphoreType.DMA((slots,)),
        ],
        compiler_params=pltpu.CompilerParams(vmem_limit_bytes=held + given + 4 * 2**20),
        name="band_partials",
    )(slot_lists, *coeff_slots, three_centre)


LEVELS = 32767
STEPS = 64
LIFT = 30
FLOOR = -100


def encode(value):
    lead, (offsets, rows, lanes) = value.shape[:-3], value.shape[-3:]
    lifted = value * 2.0**LIFT
    top = jnp.max(jnp.abs(lifted), axis=-2, keepdims=True)
    exponent = jnp.log2(jnp.maximum(top, 2.0 ** (FLOOR + 15))) - 15.0
    exponent = jnp.floor(exponent * STEPS) + 2.0
    scaled = lifted * jnp.exp2(exponent * (-1.0 / STEPS))
    coded = jnp.clip(jnp.round(scaled), -LEVELS, LEVELS).astype(jnp.int16)
    coded = coded.reshape(lead + (offsets * rows, lanes))
    scales = exponent.astype(jnp.int16).reshape(lead + (offsets, lanes))
    blank = jnp.zeros(lead + (-offsets % 16, lanes), jnp.int16)
    return jnp.concatenate([coded, scales, blank], axis=-2)


def decode(coded, offsets, rows):
    lead, lanes = coded.shape[:-2], coded.shape[-1]
    values = coded[..., : offsets * rows, :].reshape(lead + (offsets, rows, lanes)).astype(jnp.float32)
    exponent = coded[..., offsets * rows : offsets * (rows + 1), :].astype(jnp.float32)
    scale = jnp.exp2(exponent * (1.0 / STEPS)) * 2.0**-LIFT
    return values * scale.reshape(lead + (offsets, 1, lanes))


def per_device(orb_size, aux_size, three_centre, block_lists, occupied):
    def swap(value, axis, bits):
        size = {"orb": orb_size, "aux": aux_size}[axis]
        return lax.ppermute(value, axis, [(i, i ^ bits) for i in range(size)])

    def swap_sums(value, axis, bits):
        return decode(swap(encode(value), axis, bits), *value.shape[-3:-1])

    slots = {1: swap(occupied, "orb", 1)}
    slots[0] = swap(slots[1], "orb", 1)
    for s in range(2, orb_size, 2):
        slots[s] = swap(occupied, "orb", s)
    slots[2], slot_lists = lax.optimization_barrier((slots[2], block_lists ^ lax.axis_index("orb")))
    for s in range(2, orb_size, 2):
        slots[s + 1] = swap(slots[s], "orb", 1)
    keep, send = band_partials(slot_lists, [slots[s] for s in range(orb_size)], three_centre, aux_size)

    summed = keep + swap(send, "orb", 1)
    bits = list(range(1, orb_size.bit_length() - 1))
    halves = []
    for part in range(2):
        taken = summed[:, part * (aux_size // 2) : (part + 1) * (aux_size // 2)]
        taken = taken.reshape((2,) * len(bits) + taken.shape[1:])
        left = bits[::-1]
        for bit in bits if part == 0 else left[:]:
            axis = left.index(bit)
            kept = lax.index_in_dim(taken, 0, axis, keepdims=False)
            taken = kept + swap_sums(lax.index_in_dim(taken, 1, axis, keepdims=False), "orb", 1 << bit)
            left.remove(bit)
        halves.append(taken)
    rows = jnp.concatenate(halves, axis=0)
    rows = sum((swap_sums(rows[g : g + 1], "aux", g) for g in range(1, aux_size)), rows[:1])
    return jnp.transpose(rows, (0, 2, 1, 3)).reshape(1, rows.shape[2], rows.shape[1] * rows.shape[3])


def solution(mesh):
    return jax.shard_map(
        functools.partial(per_device, mesh.shape["orb"], mesh.shape["aux"]),
        mesh=mesh,
        in_specs=(
            P(("aux", "orb"), None, None, None, None, None),
            P(("aux", "orb"), None),
            P("orb", None),
        ),
        out_specs=P("orb", "aux", None),
        check_vma=False,
    )
```
